32 devices in a mesh: blk: 16 (over z, y, core), help: 2 (over x).
Axes of the slice: x: 2, y: 2, z: 4, core: 2. Of those that a mesh axis runs over, the one named last changes fastest.
Arguments:
- heads: float32 [4096, 400], P(('blk', 'help')), may hold values from -6 to 6
- tails: float32 [4096, 400], P(('blk', 'help')), may hold values from -6 to 6
- head_acc: float32 [4096], P(('blk', 'help')), may hold values from 0.01 to 0.1
- tail_acc: float32 [4096], P(('blk', 'help')), may hold values from 0.01 to 0.1
- relations: bfloat16 [7424, 400], replicated, may hold values from -0.59765625 to 0.59765625
- counts: int32 [4, 32], P(None, ('blk', 'help')), may hold values from 1 to 5, as said below
- rel_ids: int32 [4, 32, 5], P(None, ('blk', 'help')), may hold values from 0 to 7423
- head_edges: int32 [4, 32, 5, 1024], P(None, ('blk', 'help')), may hold values from 0 to 127
- tail_edges: int32 [4, 32, 5, 1024], P(None, ('blk', 'help')), may hold values from 0 to 127
Outputs:
- new_heads: float32 [4096, 400], P(('blk', 'help'))
- new_tails: float32 [4096, 400], P(('blk', 'help'))
- new_head_acc: float32 [4096], P(('blk', 'help'))
- new_tail_acc: float32 [4096], P(('blk', 'help'))
The draws below stay inside these ranges and needn't reach their ends.
Inputs may be any that keep to these rules, and one draw needn't show every extreme that they name: `counts`: in every round the two partitions 2 q and 2 q + 1 have one count from 3 to 5 and the other 1 or 2; in every round partitions 0 and 1 hold 5 and 1.
All inputs are finite; a program needn't handle non-finite values.
Results may differ from the reference program's by a relative error of at most 0.0003.
Values sent between devices are 32-bit elements; how exact they have to be, the bound alone decides.
A program may use at most 64 MiB of HBM per device.

```python
import math
from functools import partial
import jax
import jax.numpy as jnp
from jax import lax

D = 400
RELS = 7424
ROWS = 128
EDGES = 1024
MAXT = 5
ROUNDS = 4
PARTITIONS = 32
ENT = 4096
N_BLK = 16
N_HELP = 2


def draw_counts(key, part):
    keys = jax.random.split(jax.random.fold_in(key, 7), 3)
    pair_count = PARTITIONS // 2
    high = jax.random.randint(keys[0], (ROUNDS, pair_count), 3, MAXT + 1)
    low = jax.random.randint(keys[1], (ROUNDS, pair_count), 1, 3)
    high = high.at[:, 0].set(MAXT)
    low = low.at[:, 0].set(1)
    flip = jax.random.randint(keys[2], (ROUNDS, pair_count), 0, 2)
    flip = flip.at[:, 0].set(1)
    first_part = jnp.where(flip == 1, high, low)
    second_part = jnp.where(flip == 1, low, high)
    return jnp.stack([first_part, second_part], axis=-1).reshape(ROUNDS, PARTITIONS).astype(jnp.int32)


def set_ends(entries, key, smallest, largest):
    longest = entries.shape.index(max(entries.shape))
    spots = []
    for shift in (0, 1):
        where = [jax.random.randint(jax.random.fold_in(key, axis), (), 0, length) for axis, length in enumerate(entries.shape)]
        where[longest] = (where[longest] + shift) % entries.shape[longest]
        spots.append(tuple(where))
    return entries.at[spots[0]].set(smallest).at[spots[1]].set(largest)


def block_levels(own_key, dims, cuts, smallest, largest):
    loudness, own = 1.0, jax.random.fold_in(own_key, 6)
    for axis_at, shards_of in cuts:
        draws = jnp.exp(jax.random.uniform(jax.random.fold_in(own, axis_at), (shards_of,), jnp.float32, smallest / len(cuts), largest / len(cuts)))
        loudness = loudness * jnp.repeat(draws, dims[axis_at] // shards_of).reshape([-1 if axis == axis_at else 1 for axis in range(len(dims))])
    return loudness


def bell_draw(stream_key, shape, deviation, limit, cuts=(), kind=jnp.bfloat16):
    values = jax.random.normal(stream_key, shape, jnp.float32) * deviation
    if len(cuts) > 0:
        values = block_levels(stream_key, shape, cuts, -0.22, 0.18) * values
    return jnp.clip(values, min=-limit, max=limit).astype(kind)


def setup_inputs(seed: int = 0) -> dict:
    seeds = jax.random.split(jax.random.key(seed), 10)
    return {
        "heads": bell_draw(seeds[0], (ENT, D), 1.0, 6.0, ((0, 32),), jnp.float32),
        "tails": bell_draw(seeds[1], (ENT, D), 1.0, 6.0, ((0, 32),), jnp.float32),
        "head_acc": jnp.clip(jnp.exp(math.log(0.1) - 2.3025851 * jax.random.uniform(seeds[2], (ENT,), jnp.float32) ** block_levels(seeds[2], (ENT,), ((0, 32),), -0.2, 0.2)), 0.01, 0.1),
        "tail_acc": jnp.clip(jnp.exp(math.log(0.1) - 2.3025851 * jax.random.uniform(seeds[3], (ENT,), jnp.float32) ** block_levels(seeds[3], (ENT,), ((0, 32),), -0.2, 0.2)), 0.01, 0.1),
        "relations": bell_draw(seeds[4], (RELS, D), 0.1, 0.59765625),
        "counts": draw_counts(jax.random.fold_in(seeds[9], 71), 0),
        "rel_ids": set_ends(jax.random.randint(seeds[6], (ROUNDS, PARTITIONS, MAXT), 0, RELS), jax.random.fold_in(seeds[6], 1), 0, RELS - 1).astype(jnp.int32),
        "head_edges": set_ends(jax.random.randint(seeds[7], (ROUNDS, PARTITIONS, MAXT, EDGES), 0, ROWS), jax.random.fold_in(seeds[7], 1), 0, ROWS - 1).astype(jnp.int32),
        "tail_edges": set_ends(jax.random.randint(seeds[8], (ROUNDS, PARTITIONS, MAXT, EDGES), 0, ROWS), jax.random.fold_in(seeds[8], 1), 0, ROWS - 1).astype(jnp.int32),
    }


NEG_WEIGHT = 0.0625
LEARN_RATE = 0.1
HIGH = lax.Precision.HIGHEST

def task_grads(head_block, tail_block, rel_vec, head_index, tail_index):
    row_count = head_block.shape[0]
    scaled = head_block * rel_vec[None, :]
    scores = lax.dot_general(scaled, tail_block, (((1,), (1,)), ((), ())), precision=HIGH, preferred_element_type=jnp.float32)
    labels = jnp.zeros((row_count, row_count), jnp.float32).at[head_index, tail_index].add(1.0)
    coefficient = NEG_WEIGHT * jax.nn.sigmoid(scores) - labels
    head_grad = jnp.dot(coefficient, tail_block, precision=HIGH, preferred_element_type=jnp.float32) * rel_vec[None, :]
    tail_grad = lax.dot_general(coefficient, scaled, (((0,), (0,)), ((), ())), precision=HIGH, preferred_element_type=jnp.float32)
    return (head_grad, tail_grad)

def adagrad(block, state, grad):
    new_state = state + lax.optimization_barrier(jnp.mean(grad * grad, axis=1))
    return (block - LEARN_RATE * grad / jnp.sqrt(new_state)[:, None], new_state)

def bucket(packed, relations):
    head_block, tail_block, head_state, tail_state, task_count, rel_row, head_rows, tail_rows = packed

    def add_task(slot_id, totals):
        rel_vec = relations[rel_row[slot_id]].astype(jnp.float32)
        head_grad, tail_grad = task_grads(head_block, tail_block, rel_vec, head_rows[slot_id], tail_rows[slot_id])
        return (totals[0] + head_grad, totals[1] + tail_grad)
    empty = jnp.zeros(head_block.shape, jnp.float32)
    head_grad, tail_grad = lax.fori_loop(jnp.int32(0), task_count.astype(jnp.int32), add_task, (empty, empty))
    new_head, new_head_state = adagrad(head_block, head_state, head_grad)
    new_tail, new_tail_state = adagrad(tail_block, tail_state, tail_grad)
    return (new_head, new_tail, new_head_state, new_tail_state)

def reference(heads, tails, head_acc, tail_acc, relations, counts, rel_ids, head_edges, tail_edges):
    head_grid = heads.reshape(N_BLK, N_HELP, ROWS, D)
    tail_grid = tails.reshape(N_BLK, N_HELP, ROWS, D)
    head_state = head_acc.reshape(N_BLK, N_HELP, ROWS)
    tail_state = tail_acc.reshape(N_BLK, N_HELP, ROWS)
    for round_ix in range(ROUNDS):
        tail_here = jnp.roll(tail_grid, round_ix, axis=0).reshape(PARTITIONS, ROWS, D)
        state_here = jnp.roll(tail_state, round_ix, axis=0).reshape(PARTITIONS, ROWS)
        outcome = lax.map(partial(bucket, relations=relations), (head_grid.reshape(PARTITIONS, ROWS, D), tail_here, head_state.reshape(PARTITIONS, ROWS), state_here, counts[round_ix], rel_ids[round_ix], head_edges[round_ix], tail_edges[round_ix]))
        head_grid = outcome[0].reshape(N_BLK, N_HELP, ROWS, D)
        tail_grid = jnp.roll(outcome[1].reshape(N_BLK, N_HELP, ROWS, D), -round_ix, axis=0)
        head_state = outcome[2].reshape(N_BLK, N_HELP, ROWS)
        tail_state = jnp.roll(outcome[3].reshape(N_BLK, N_HELP, ROWS), -round_ix, axis=0)
    return (head_grid.reshape(ENT, D), tail_grid.reshape(ENT, D), head_state.reshape(ENT), tail_state.reshape(ENT))
```

```python
import functools

import jax
import jax.numpy as jnp
from jax import lax
from jax.experimental import pallas as pl
from jax.experimental.pallas import tpu as pltpu
from jax.sharding import PartitionSpec as P

NEG_WEIGHT = 0.0625
LEARN_RATE = 0.1
LANES = 128
SUBLANES = 8
NT = (((1,), (1,)), ((), ()))
NN = (((1,), (0,)), ((), ()))


def split(value):
    high = value.astype(jnp.bfloat16)
    return high, (value - high.astype(jnp.float32)).astype(jnp.bfloat16)


def product(left, right, dims):
    def dot(a, b):
        return lax.dot_general(a, b, dims, preferred_element_type=jnp.float32)

    return dot(left[0], right[0]) + (dot(left[0], right[1]) + dot(left[1], right[0]))


def task(s, rows):
    return slice(s * rows, (s + 1) * rows)


def one_hot(index, rows):
    row_of = lax.broadcasted_iota(jnp.int32, (rows, index.shape[1]), 0)
    return jnp.where(row_of == index, 1.0, 0.0).astype(jnp.bfloat16)


def label_counts(head_index, tail_index, rows):
    return lax.dot_general(
        one_hot(tail_index, rows),
        one_hot(head_index, rows),
        NT,
        preferred_element_type=jnp.float32,
    )


def prepare(
    counts_ref,
    rel_ids_ref,
    head_edges_ref,
    tail_edges_ref,
    relations_ref,
    gathered_ref,
    active_ref,
    labels_ref,
    groups,
    sems,
):
    rounds = counts_ref.shape[1]
    slots = rel_ids_ref.shape[2]
    rows = labels_ref.shape[0]
    copies = []
    for at in range(rounds * slots):
        rel_id = rel_ids_ref[at // slots, 0, at % slots]
        start = pl.multiple_of(lax.div(rel_id, LANES) * LANES, LANES)
        copy = pltpu.make_async_copy(
            relations_ref.at[:, pl.ds(start, LANES)], groups.at[at], sems.at[at]
        )
        copy.start()
        copies.append(copy)
    task_of = lax.broadcasted_iota(jnp.int32, (1, slots * rows), 1) // rows
    for k in range(rounds):
        active_ref[k : k + 1, :] = jnp.where(task_of < counts_ref[0, k], 1.0, 0.0)
    for s in range(slots):
        labels_ref[:, task(s, rows)] = label_counts(head_edges_ref[s], tail_edges_ref[s], rows)
    lane_from = lax.broadcasted_iota(jnp.int32, (LANES, LANES), 0)
    lane_to = lax.broadcasted_iota(jnp.int32, (LANES, LANES), 1)
    total = jnp.zeros(gathered_ref.shape, jnp.float32)
    for at, copy in enumerate(copies):
        lane = lax.rem(rel_ids_ref[at // slots, 0, at % slots], LANES)
        pick = jnp.where((lane_from == lane) & (lane_to == at), 1.0, 0.0).astype(jnp.bfloat16)
        copy.wait()
        total = total + jnp.dot(groups[at], pick, preferred_element_type=jnp.float32)
    gathered_ref[...] = total.astype(jnp.bfloat16)


def kernel(
    blk_size,
    slots,
    heads_ref,
    tails_ref,
    head_acc_ref,
    tail_acc_ref,
    head_edges_ref,
    tail_edges_ref,
    gathered_ref,
    active_ref,
    first_labels_ref,
    new_heads_ref,
    new_tails_ref,
    new_head_acc_ref,
    new_tail_acc_ref,
    spread_rel,
    labels,
    scaled_high,
    scaled_low,
    arrived,
    leaving,
    send_sem,
    recv_sem,
):
    width, rows = heads_ref.shape
    rounds = active_ref.shape[0]
    me = lax.axis_index("blk")

    def device(distance):
        return lax.rem(me + distance + blk_size, blk_size)

    barrier = pltpu.get_barrier_semaphore()
    partners = (1, -1, rounds - 1, 1 - rounds)
    for distance in partners:
        pl.semaphore_signal(
            barrier,
            inc=1,
            device_id={"blk": device(distance)},
            device_id_type=pl.DeviceIdType.MESH,
        )

    def store_labels(k):
        for s in range(slots):
            at = k * slots + s
            labels[:, task(s, rows)] = label_counts(head_edges_ref[at], tail_edges_ref[at], rows)

    def store_scaled(k, head_block):
        for s in range(slots):
            lane_of = lax.broadcasted_iota(jnp.int32, (LANES, rows), 0)
            pick = jnp.where(lane_of == k * slots + s, 1.0, 0.0).astype(jnp.bfloat16)
            rel = jnp.dot(gathered_ref[...], pick, preferred_element_type=jnp.float32)
            spread_rel[k % 2, :, task(s, rows)] = rel
            high, low = split(head_block * rel)
            scaled_high[:, task(s, rows)] = high
            scaled_low[:, task(s, rows)] = low

    def adagrad(block, state, grad):
        state = state + jnp.sum(grad * grad, axis=0, keepdims=True) * (1.0 / width)
        return block - grad * (LEARN_RATE / jnp.sqrt(state)), state

    store_scaled(0, heads_ref[...])
    head_state = head_acc_ref[...]
    pl.semaphore_wait(barrier, len(partners))

    copies = []
    for k in range(rounds):
        if k == 0:
            tail_block = tails_ref[...]
            tail_state = tail_acc_ref[...]
        else:
            copies[k - 1].wait_recv()
            tail_block = arrived[k - 1, :width, :]
            tail_state = arrived[k - 1, width : width + 1, :]
        scaled = (scaled_high[...], scaled_low[...])
        scores = product(split(jnp.transpose(tail_block)), scaled, NN)
        active = active_ref[k : k + 1, :]
        counted = first_labels_ref[...] if k == 0 else labels[...]
        weight = active * (0.5 * NEG_WEIGHT)
        coefficient = weight * jnp.tanh(0.5 * scores) + (weight - active * counted)
        coefficient = split(coefficient)
        tail_grad = product(scaled, coefficient, NT)
        new_tail, new_state = adagrad(tail_block, tail_state, tail_grad)
        leaving[k, :width, :] = new_tail
        leaving[k, width:, :] = jnp.broadcast_to(new_state, (SUBLANES, rows))
        copy = pltpu.make_async_remote_copy(
            src_ref=leaving.at[k],
            dst_ref=arrived.at[k],
            send_sem=send_sem.at[k],
            recv_sem=recv_sem.at[k],
            device_id={"blk": device(1 if k < rounds - 1 else 1 - rounds)},
            device_id_type=pl.DeviceIdType.MESH,
        )
        copy.start()
        copies.append(copy)

        weighted = product(split(tail_block), coefficient, NN) * spread_rel[k % 2]
        head_grad = weighted[:, task(0, rows)]
        for s in range(1, slots):
            head_grad = head_grad + weighted[:, task(s, rows)]
        old_head = heads_ref[...] if k == 0 else new_heads_ref[...]
        new_head, head_state = adagrad(old_head, head_state, head_grad)
        new_heads_ref[...] = new_head
        if k < rounds - 1:
            store_scaled(k + 1, new_head)
            store_labels(k + 1)

    new_head_acc_ref[...] = head_state
    copies[-1].wait_recv()
    new_tails_ref[...] = arrived[rounds - 1, :width, :]
    new_tail_acc_ref[...] = arrived[rounds - 1, width : width + 1, :]
    for copy in copies:
        copy.wait_send()


def on_device(
    blk_size, heads, tails, head_acc, tail_acc, relations, counts, rel_ids, head_edges, tail_edges
):
    rows, width = heads.shape
    rounds, _, slots, edges = head_edges.shape
    vmem = pl.BlockSpec(memory_space=pltpu.VMEM)
    smem = pl.BlockSpec(memory_space=pltpu.SMEM)
    head_edges = head_edges.reshape(rounds * slots, 1, edges)
    tail_edges = tail_edges.reshape(rounds * slots, 1, edges)
    gathered, active, first_labels = pl.pallas_call(
        prepare,
        out_shape=(
            jax.ShapeDtypeStruct((width, LANES), jnp.bfloat16),
            jax.ShapeDtypeStruct((rounds, slots * rows), jnp.float32),
            jax.ShapeDtypeStruct((rows, slots * rows), jnp.float32),
        ),
        in_specs=[smem, smem, vmem, vmem, pl.BlockSpec(memory_space=pl.ANY)],
        out_specs=(vmem, vmem, vmem),
        scratch_shapes=[
            pltpu.VMEM((rounds * slots, width, LANES), jnp.bfloat16),
            pltpu.SemaphoreType.DMA((rounds * slots,)),
        ],
        compiler_params=pltpu.CompilerParams(vmem_limit_bytes=24 * 1024 * 1024),
    )(counts.T, rel_ids, head_edges, tail_edges, relations.T)
    new_heads, new_tails, new_head_acc, new_tail_acc = pl.pallas_call(
        functools.partial(kernel, blk_size, slots),
        out_shape=(
            jax.ShapeDtypeStruct((width, rows), jnp.float32),
            jax.ShapeDtypeStruct((width, rows), jnp.float32),
            jax.ShapeDtypeStruct((1, rows), jnp.float32),
            jax.ShapeDtypeStruct((1, rows), jnp.float32),
        ),
        in_specs=[vmem] * 9,
        out_specs=(vmem, vmem, vmem, vmem),
        scratch_shapes=[
            pltpu.VMEM((2, width, slots * rows), jnp.float32),
            pltpu.VMEM((rows, slots * rows), jnp.float32),
            pltpu.VMEM((width, slots * rows), jnp.bfloat16),
            pltpu.VMEM((width, slots * rows), jnp.bfloat16),
            pltpu.VMEM((rounds, width + SUBLANES, rows), jnp.float32),
            pltpu.VMEM((rounds, width + SUBLANES, rows), jnp.float32),
            pltpu.SemaphoreType.DMA((rounds,)),
            pltpu.SemaphoreType.DMA((rounds,)),
        ],
        compiler_params=pltpu.CompilerParams(
            collective_id=0, has_side_effects=True, vmem_limit_bytes=48 * 1024 * 1024
        ),
    )(
        heads.T,
        tails.T,
        head_acc.reshape(1, rows),
        tail_acc.reshape(1, rows),
        head_edges,
        tail_edges,
        gathered,
        active,
        first_labels,
    )
    return (new_heads.T, new_tails.T, new_head_acc.reshape(rows), new_tail_acc.reshape(rows))


def solution(mesh):
    both = ("blk", "help")
    in_specs = (
        P(both, None),
        P(both, None),
        P(both),
        P(both),
        P(),
        P(None, both),
        P(None, both, None),
        P(None, both, None, None),
        P(None, both, None, None),
    )
    out_specs = (P(both, None), P(both, None), P(both), P(both))
    return jax.shard_map(
        functools.partial(on_device, mesh.shape["blk"]),
        mesh=mesh,
        in_specs=in_specs,
        out_specs=out_specs,
        check_vma=False,
    )
```

```python
import functools

import jax
import jax.numpy as jnp
from jax import lax
from jax.experimental import pallas as pl
from jax.experimental.pallas import tpu as pltpu
from jax.sharding import PartitionSpec as P

NEG_WEIGHT = 0.0625
LEARN_RATE = 0.1
LANES = 128
SUBLANES = 8
FIRST_PART = 256
VMEM_BYTES = 60 * 1024 * 1024
NT = (((1,), (1,)), ((), ()))
NN = (((1,), (0,)), ((), ()))


def split(value):
    high = value.astype(jnp.bfloat16)
    return high, (value - high.astype(jnp.float32)).astype(jnp.bfloat16)


def dot(left, right, dims=NN):
    return lax.dot_general(left, right, dims, preferred_element_type=jnp.float32)


def product(left, right):
    return dot(left[0], right[0]) + (dot(left[0], right[1]) + dot(left[1], right[0]))


def task(s, rows):
    return slice(s * rows, (s + 1) * rows)


def one_hot(index, rows):
    row_of = lax.broadcasted_iota(jnp.int32, (rows, index.shape[1]), 0)
    same = row_of.astype(jnp.bfloat16) == index.astype(jnp.bfloat16)
    return jnp.where(same, jnp.bfloat16(1.0), jnp.bfloat16(0.0))


def label_counts(head_index, tail_index, rows):
    return dot(one_hot(tail_index, rows), one_hot(head_index, rows), NT)


def prepare(
    counts_hbm,
    rel_ids_hbm,
    head_edges_hbm,
    tail_edges_hbm,
    relations_ref,
    heads_hbm,
    tails_hbm,
    gathered_ref,
    active_ref,
    labels_ref,
    heads_ref,
    tails_ref,
    counts_ref,
    rel_ids_ref,
    head_edges_ref,
    tail_edges_ref,
    groups,
    sems,
    input_sems,
):
    rounds = counts_ref.shape[1]
    slots = rel_ids_ref.shape[2]
    rows = labels_ref.shape[0]
    inputs = (
        (rel_ids_hbm, rel_ids_ref),
        (counts_hbm, counts_ref),
        (head_edges_hbm.at[pl.ds(0, slots)], head_edges_ref),
        (tail_edges_hbm.at[pl.ds(0, slots)], tail_edges_ref),
        (heads_hbm, heads_ref),
        (tails_hbm, tails_ref),
    )
    input_copies = []
    for at, (source, target) in enumerate(inputs):
        copy = pltpu.make_async_copy(source, target, input_sems.at[at])
        copy.start()
        input_copies.append(copy)
    input_copies[0].wait()
    copies = []
    for at in range(rounds * slots):
        rel_id = rel_ids_ref[at // slots, 0, at % slots]
        start = pl.multiple_of(lax.div(rel_id, LANES) * LANES, LANES)
        copy = pltpu.make_async_copy(
            relations_ref.at[:, pl.ds(start, LANES)], groups.at[at], sems.at[at]
        )
        copy.start()
        copies.append(copy)
    for copy in input_copies[1:]:
        copy.wait()
    task_of = lax.broadcasted_iota(jnp.int32, (1, slots * rows), 1) // rows
    for k in range(rounds):
        active_ref[k : k + 1, :] = jnp.where(task_of < counts_ref[0, k], 1.0, 0.0)
    for s in range(slots):
        labels_ref[:, task(s, rows)] = label_counts(head_edges_ref[s], tail_edges_ref[s], rows)
    lane_from = lax.broadcasted_iota(jnp.int32, (LANES, LANES), 0)
    lane_to = lax.broadcasted_iota(jnp.int32, (LANES, LANES), 1)
    total = jnp.zeros(gathered_ref.shape, jnp.float32)
    for at in range(0, rounds * slots, 2):
        pair = range(at, min(at + 2, rounds * slots))
        picks = []
        for one in pair:
            lane = lax.rem(rel_ids_ref[one // slots, 0, one % slots], LANES)
            pick = jnp.where((lane_from == lane) & (lane_to == one), 1.0, 0.0)
            picks.append(pick.astype(jnp.bfloat16))
            copies[one].wait()
        group = jnp.concatenate([groups[one] for one in pair], axis=1)
        total = total + dot(group, jnp.concatenate(picks, axis=0))
    gathered_ref[...] = total.astype(jnp.bfloat16)


def kernel(
    blk_size,
    slots,
    heads_ref,
    tails_ref,
    gathered_ref,
    active_ref,
    first_labels_ref,
    head_acc_hbm,
    tail_acc_hbm,
    head_edges_hbm,
    tail_edges_hbm,
    new_heads_ref,
    new_tails_ref,
    new_head_acc_ref,
    new_tail_acc_ref,
    head_acc_ref,
    tail_acc_ref,
    head_edges_ref,
    tail_edges_ref,
    spread_rel,
    labels,
    scaled_high,
    scaled_low,
    arrived,
    leaving,
    input_sems,
    send_sem,
    recv_sem,
):
    width, rows = heads_ref.shape
    rounds = active_ref.shape[0]
    padded = width + SUBLANES
    parts = ((0, FIRST_PART), (FIRST_PART, padded))
    me = lax.axis_index("blk")

    def device(distance):
        return lax.rem(me + distance + blk_size, blk_size)

    barrier = pltpu.get_barrier_semaphore()
    partners = (1, -1, rounds - 1, 1 - rounds)
    for distance in partners:
        pl.semaphore_signal(
            barrier,
            inc=1,
            device_id={"blk": device(distance)},
            device_id_type=pl.DeviceIdType.MESH,
        )

    inputs = (
        (head_acc_hbm, head_acc_ref),
        (tail_acc_hbm, tail_acc_ref),
        (head_edges_hbm, head_edges_ref),
        (tail_edges_hbm, tail_edges_ref),
    )
    input_copies = []
    for at, (source, target) in enumerate(inputs):
        copy = pltpu.make_async_copy(source, target, input_sems.at[at])
        copy.start()
        input_copies.append(copy)

    def store_labels(k):
        for s in range(slots):
            at = k * slots + s
            labels[:, task(s, rows)] = label_counts(head_edges_ref[at], tail_edges_ref[at], rows)

    def store_scaled(k, head_block):
        lane_of = lax.broadcasted_iota(jnp.int32, (LANES, slots * rows), 0)
        task_of = lax.broadcasted_iota(jnp.int32, (LANES, slots * rows), 1) // rows
        pick = jnp.where(lane_of == k * slots + task_of, 1.0, 0.0).astype(jnp.bfloat16)
        spread = dot(gathered_ref[...], pick)
        spread_rel[k % 2] = spread
        for s in range(slots):
            high, low = split(head_block * spread[:, task(s, rows)])
            scaled_high[:, task(s, rows)] = high
            scaled_low[:, task(s, rows)] = low

    def state_after(state, grad):
        return state + jnp.sum(grad * grad, axis=0, keepdims=True) * (1.0 / width)

    store_scaled(0, heads_ref[...])
    for copy in input_copies:
        copy.wait()
    head_state = head_acc_ref[...]
    pl.semaphore_wait(barrier, len(partners))

    copies = []
    for k in range(rounds):
        scores = None
        pieces = []
        for at, (start, stop) in enumerate(parts):
            end = min(stop, width)
            if k == 0:
                piece = tails_ref[start:end, :]
            else:
                copies[2 * (k - 1) + at].wait_recv()
                piece = arrived[k - 1, start:end, :]
            scaled_part = (scaled_high[start:end, :], scaled_low[start:end, :])
            partial = product(split(jnp.transpose(piece)), scaled_part)
            scores = partial if scores is None else scores + partial
            pieces.append(piece)
        tail_state = tail_acc_ref[...] if k == 0 else arrived[k - 1, width : width + 1, :]
        active = active_ref[k : k + 1, :]
        counted = first_labels_ref[...] if k == 0 else labels[...]
        weight = active * (0.5 * NEG_WEIGHT)
        coefficient = weight * jnp.tanh(0.5 * scores) + (weight - active * counted)
        high, low = split(coefficient)
        both = dot(scaled_high[...], jnp.concatenate([high, low], axis=0), NT)
        tail_grad = both[:, :rows] + (both[:, rows:] + dot(scaled_low[...], high, NT))
        tail_state = state_after(tail_state, tail_grad)
        rate = LEARN_RATE / jnp.sqrt(tail_state)
        for at, (start, stop) in enumerate(parts):
            end = min(stop, width)
            leaving[k, start:end, :] = pieces[at] - tail_grad[start:end] * rate
            if stop > width:
                leaving[k, width:, :] = jnp.broadcast_to(tail_state, (SUBLANES, rows))
            copy = pltpu.make_async_remote_copy(
                src_ref=leaving.at[k, pl.ds(start, stop - start)],
                dst_ref=arrived.at[k, pl.ds(start, stop - start)],
                send_sem=send_sem.at[k, at],
                recv_sem=recv_sem.at[k, at],
                device_id={"blk": device(1 if k < rounds - 1 else 1 - rounds)},
                device_id_type=pl.DeviceIdType.MESH,
            )
            copy.start()
            copies.append(copy)

        tail_high, tail_low = split(jnp.concatenate(pieces, axis=0))
        wide = jnp.concatenate([tail_high, tail_low, tail_high], axis=1)
        tall = jnp.concatenate([high, high, low], axis=0)
        weighted = dot(wide, tall) * spread_rel[k % 2]
        head_grad = weighted[:, task(0, rows)]
        for s in range(1, slots):
            head_grad = head_grad + weighted[:, task(s, rows)]
        old_head = heads_ref[...] if k == 0 else new_heads_ref[...]
        head_state = state_after(head_state, head_grad)
        new_head = old_head - head_grad * (LEARN_RATE / jnp.sqrt(head_state))
        new_heads_ref[...] = new_head
        if k < rounds - 1:
            store_scaled(k + 1, new_head)
            store_labels(k + 1)

    new_head_acc_ref[...] = head_state
    for copy in copies[-2:]:
        copy.wait_recv()
    new_tails_ref[...] = arrived[rounds - 1, :width, :]
    new_tail_acc_ref[...] = arrived[rounds - 1, width : width + 1, :]
    for copy in copies:
        copy.wait_send()


def write_out(*refs):
    sems = refs[-1]
    half = (len(refs) - 1) // 2
    copies = []
    for at in range(half):
        copy = pltpu.make_async_copy(refs[at], refs[half + at], sems.at[at])
        copy.start()
        copies.append(copy)
    for copy in copies:
        copy.wait()


def on_device(
    blk_size, heads, tails, head_acc, tail_acc, relations, counts, rel_ids, head_edges, tail_edges
):
    rows, width = heads.shape
    rounds, _, slots, edges = head_edges.shape
    vmem = pl.BlockSpec(memory_space=pltpu.VMEM)
    hbm = pl.BlockSpec(memory_space=pltpu.HBM)
    block = jax.ShapeDtypeStruct((width, rows), jnp.float32)
    line = jax.ShapeDtypeStruct((1, rows), jnp.float32)
    head_edges = head_edges.reshape(rounds * slots, 1, edges)
    tail_edges = tail_edges.reshape(rounds * slots, 1, edges)
    gathered, active, first_labels, heads_near, tails_near = pl.pallas_call(
        prepare,
        out_shape=(
            jax.ShapeDtypeStruct((width, LANES), jnp.bfloat16),
            jax.ShapeDtypeStruct((rounds, slots * rows), jnp.float32),
            jax.ShapeDtypeStruct((rows, slots * rows), jnp.float32),
            block,
            block,
        ),
        in_specs=[hbm] * 7,
        out_specs=(vmem,) * 5,
        scratch_shapes=[
            pltpu.SMEM((1, rounds), jnp.int32),
            pltpu.SMEM((rounds, 1, slots), jnp.int32),
            pltpu.VMEM((slots, 1, edges), jnp.int32),
            pltpu.VMEM((slots, 1, edges), jnp.int32),
            pltpu.VMEM((rounds * slots, width, LANES), jnp.bfloat16),
            pltpu.SemaphoreType.DMA((rounds * slots,)),
            pltpu.SemaphoreType.DMA((6,)),
        ],
        compiler_params=pltpu.CompilerParams(vmem_limit_bytes=VMEM_BYTES),
    )(counts.T, rel_ids, head_edges, tail_edges, relations.T, heads.T, tails.T)
    results = pl.pallas_call(
        functools.partial(kernel, blk_size, slots),
        out_shape=(block, block, line, line),
        in_specs=[vmem] * 5 + [hbm] * 4,
        out_specs=(vmem,) * 4,
        scratch_shapes=[
            pltpu.VMEM((1, rows), jnp.float32),
            pltpu.VMEM((1, rows), jnp.float32),
            pltpu.VMEM((rounds * slots, 1, edges), jnp.int32),
            pltpu.VMEM((rounds * slots, 1, edges), jnp.int32),
            pltpu.VMEM((2, width, slots * rows), jnp.float32),
            pltpu.VMEM((rows, slots * rows), jnp.float32),
            pltpu.VMEM((width, slots * rows), jnp.bfloat16),
            pltpu.VMEM((width, slots * rows), jnp.bfloat16),
            pltpu.VMEM((rounds, width + SUBLANES, rows), jnp.float32),
            pltpu.VMEM((rounds, width + SUBLANES, rows), jnp.float32),
            pltpu.SemaphoreType.DMA((4,)),
            pltpu.SemaphoreType.DMA((rounds, 2)),
            pltpu.SemaphoreType.DMA((rounds, 2)),
        ],
        compiler_params=pltpu.CompilerParams(
            collective_id=0, has_side_effects=True, vmem_limit_bytes=VMEM_BYTES
        ),
    )(
        heads_near,
        tails_near,
        gathered,
        active,
        first_labels,
        head_acc.reshape(1, rows),
        tail_acc.reshape(1, rows),
        head_edges,
        tail_edges,
    )
    new_heads, new_tails, new_head_acc, new_tail_acc = pl.pallas_call(
        write_out,
        out_shape=(block, block, line, line),
        in_specs=[hbm] * 4,
        out_specs=(hbm,) * 4,
        scratch_shapes=[pltpu.SemaphoreType.DMA((4,))],
        compiler_params=pltpu.CompilerParams(vmem_limit_bytes=VMEM_BYTES),
    )(*results)
    return (new_heads.T, new_tails.T, new_head_acc.reshape(rows), new_tail_acc.reshape(rows))


def solution(mesh):
    both = ("blk", "help")
    in_specs = (
        P(both, None),
        P(both, None),
        P(both),
        P(both),
        P(),
        P(None, both),
        P(None, both, None),
        P(None, both, None, None),
        P(None, both, None, None),
    )
    out_specs = (P(both, None), P(both, None), P(both), P(both))
    return jax.shard_map(
        functools.partial(on_device, mesh.shape["blk"]),
        mesh=mesh,
        in_specs=in_specs,
        out_specs=out_specs,
        check_vma=False,
    )
```

```python
import functools

import jax
import jax.numpy as jnp
from jax import lax
from jax.experimental import pallas as pl
from jax.experimental.pallas import tpu as pltpu
from jax.sharding import PartitionSpec as P

NEG_WEIGHT = 0.0625
LEARN_RATE = 0.1
LANES = 128
SUBLANES = 8
FIRST_PART = 256
TABLE_PARTS = 4
VMEM_BYTES = 60 * 1024 * 1024
NT = (((1,), (1,)), ((), ()))
NN = (((1,), (0,)), ((), ()))


def split(value):
    high = value.astype(jnp.bfloat16)
    return high, (value - high.astype(jnp.float32)).astype(jnp.bfloat16)


def dot(left, right, dims=NN):
    return lax.dot_general(left, right, dims, preferred_element_type=jnp.float32)


def product(left, right):
    return dot(left[0], right[0]) + (dot(left[0], right[1]) + dot(left[1], right[0]))


def task(s, rows):
    return slice(s * rows, (s + 1) * rows)


def one_hot(index, rows):
    row_of = lax.broadcasted_iota(jnp.int32, (rows, index.shape[1]), 0)
    same = row_of.astype(jnp.bfloat16) == index.astype(jnp.bfloat16)
    return jnp.where(same, jnp.bfloat16(1.0), jnp.bfloat16(0.0))


def label_counts(head_index, tail_index, rows):
    return dot(one_hot(tail_index, rows), one_hot(head_index, rows), NT)


def kernel(
    blk_size,
    heads_ref,
    tails_ref,
    head_acc_ref,
    tail_acc_ref,
    counts_ref,
    rel_ids_ref,
    head_edges_ref,
    tail_edges_ref,
    relations_hbm,
    new_heads_ref,
    new_tails_ref,
    new_head_acc_ref,
    new_tail_acc_ref,
    table,
    gathered,
    spread_rel,
    labels,
    scaled_high,
    scaled_low,
    arrived,
    leaving,
    table_sems,
    send_sem,
    recv_sem,
):
    width, rows = heads_ref.shape
    rounds = counts_ref.shape[1]
    slots = rel_ids_ref.shape[2]
    rels = table.shape[1]
    padded = width + SUBLANES
    parts = ((0, FIRST_PART), (FIRST_PART, padded))
    me = lax.axis_index("blk")

    def device(distance):
        return lax.rem(me + distance + blk_size, blk_size)

    step = pl.cdiv(rels, TABLE_PARTS * 2 * LANES) * 2 * LANES
    table_copies = []
    for at, start in enumerate(range(0, rels, step)):
        lanes = pl.ds(start, min(step, rels - start))
        copy = pltpu.make_async_copy(
            relations_hbm.at[:, lanes], table.at[:, lanes], table_sems.at[at]
        )
        copy.start()
        table_copies.append(copy)

    barrier = pltpu.get_barrier_semaphore()
    partners = (1, -1, rounds - 1, 1 - rounds)
    for distance in partners:
        pl.semaphore_signal(
            barrier,
            inc=1,
            device_id={"blk": device(distance)},
            device_id_type=pl.DeviceIdType.MESH,
        )

    def store_labels(k):
        for s in range(slots):
            at = k * slots + s
            labels[:, task(s, rows)] = label_counts(head_edges_ref[at], tail_edges_ref[at], rows)

    def gather_relations():
        lane = lax.broadcasted_iota(jnp.int32, (1, LANES), 1)
        wanted = jnp.full((1, LANES), -1, jnp.int32)
        for at in range(rounds * slots):
            rel_id = rel_ids_ref[at // slots, :, at % slots : at % slots + 1]
            wanted = jnp.where(lane == at, rel_id, wanted)
        total = jnp.zeros(gathered.shape, jnp.float32)
        for at, start in enumerate(range(0, rels, step)):
            size = min(step, rels - start)
            rel_of = lax.broadcasted_iota(jnp.int32, (size, LANES), 0) + start
            pick = jnp.where(rel_of == wanted, 1.0, 0.0).astype(jnp.bfloat16)
            table_copies[at].wait()
            total = total + dot(table[:, start : start + size], pick)
        gathered[...] = total.astype(jnp.bfloat16)

    def store_scaled(k, head_block):
        lane_of = lax.broadcasted_iota(jnp.int32, (LANES, slots * rows), 0)
        task_of = lax.broadcasted_iota(jnp.int32, (LANES, slots * rows), 1) // rows
        pick = jnp.where(lane_of == k * slots + task_of, 1.0, 0.0).astype(jnp.bfloat16)
        spread = dot(gathered[...], pick)
        spread_rel[k % 2] = spread
        for s in range(slots):
            high, low = split(head_block * spread[:, task(s, rows)])
            scaled_high[:, task(s, rows)] = high
            scaled_low[:, task(s, rows)] = low

    def state_after(state, grad):
        return state + jnp.sum(grad * grad, axis=0, keepdims=True) * (1.0 / width)

    store_labels(0)
    gather_relations()
    store_scaled(0, heads_ref[...])
    head_state = head_acc_ref[...]
    pl.semaphore_wait(barrier, len(partners))

    copies = []
    for k in range(rounds):
        scores = None
        pieces = []
        for at, (start, stop) in enumerate(parts):
            end = min(stop, width)
            if k == 0:
                piece = tails_ref[start:end, :]
            else:
                copies[2 * (k - 1) + at].wait_recv()
                piece = arrived[k - 1, start:end, :]
            scaled_part = (scaled_high[start:end, :], scaled_low[start:end, :])
            partial = product(split(jnp.transpose(piece)), scaled_part)
            scores = partial if scores is None else scores + partial
            pieces.append(piece)
        tail_state = tail_acc_ref[...] if k == 0 else arrived[k - 1, width : width + 1, :]
        task_of = lax.broadcasted_iota(jnp.int32, (1, slots * rows), 1) // rows
        active = jnp.where(task_of < counts_ref[:, k : k + 1], 1.0, 0.0)
        weight = active * (0.5 * NEG_WEIGHT)
        coefficient = weight * jnp.tanh(0.5 * scores) + (weight - active * labels[...])
        high, low = split(coefficient)
        both = dot(scaled_high[...], jnp.concatenate([high, low], axis=0), NT)
        tail_grad = both[:, :rows] + (both[:, rows:] + dot(scaled_low[...], high, NT))
        tail_state = state_after(tail_state, tail_grad)
        rate = LEARN_RATE / jnp.sqrt(tail_state)
        for at, (start, stop) in enumerate(parts):
            end = min(stop, width)
            leaving[k, start:end, :] = pieces[at] - tail_grad[start:end] * rate
            if stop > width:
                leaving[k, width:, :] = jnp.broadcast_to(tail_state, (SUBLANES, rows))
            copy = pltpu.make_async_remote_copy(
                src_ref=leaving.at[k, pl.ds(start, stop - start)],
                dst_ref=arrived.at[k, pl.ds(start, stop - start)],
                send_sem=send_sem.at[k, at],
                recv_sem=recv_sem.at[k, at],
                device_id={"blk": device(1 if k < rounds - 1 else 1 - rounds)},
                device_id_type=pl.DeviceIdType.MESH,
            )
            copy.start()
            copies.append(copy)

        tail_high, tail_low = split(jnp.concatenate(pieces, axis=0))
        wide = jnp.concatenate([tail_high, tail_low, tail_high], axis=1)
        tall = jnp.concatenate([high, high, low], axis=0)
        weighted = dot(wide, tall) * spread_rel[k % 2]
        head_grad = weighted[:, task(0, rows)]
        for s in range(1, slots):
            head_grad = head_grad + weighted[:, task(s, rows)]
        old_head = heads_ref[...] if k == 0 else new_heads_ref[...]
        head_state = state_after(head_state, head_grad)
        new_head = old_head - head_grad * (LEARN_RATE / jnp.sqrt(head_state))
        new_heads_ref[...] = new_head
        if k < rounds - 1:
            store_scaled(k + 1, new_head)
            store_labels(k + 1)

    new_head_acc_ref[...] = head_state
    for copy in copies[-2:]:
        copy.wait_recv()
    new_tails_ref[...] = arrived[rounds - 1, :width, :]
    new_tail_acc_ref[...] = arrived[rounds - 1, width : width + 1, :]
    for copy in copies:
        copy.wait_send()


def write_out(*refs):
    count = (len(refs) - 2) // 3
    sems_in, sems_out = refs[-2:]
    copies_in = []
    copies_out = []
    for at in range(count):
        near = refs[2 * count + at]
        copies_in.append(pltpu.make_async_copy(refs[at], near, sems_in.at[at]))
        copies_out.append(pltpu.make_async_copy(near, refs[count + at], sems_out.at[at]))
        copies_in[at].start()
    for at in range(count):
        copies_in[at].wait()
        copies_out[at].start()
    for copy in copies_out:
        copy.wait()


def on_device(
    blk_size, heads, tails, head_acc, tail_acc, relations, counts, rel_ids, head_edges, tail_edges
):
    rows, width = heads.shape
    rounds, _, slots, edges = head_edges.shape
    vmem = pl.BlockSpec(memory_space=pltpu.VMEM)
    hbm = pl.BlockSpec(memory_space=pltpu.HBM)
    block = jax.ShapeDtypeStruct((width, rows), jnp.float32)
    line = jax.ShapeDtypeStruct((1, rows), jnp.float32)
    head_edges = head_edges.reshape(rounds * slots, 1, edges)
    tail_edges = tail_edges.reshape(rounds * slots, 1, edges)
    results = pl.pallas_call(
        functools.partial(kernel, blk_size),
        out_shape=(block, block, line, line),
        in_specs=[vmem] * 8 + [hbm],
        out_specs=(vmem,) * 4,
        scratch_shapes=[
            pltpu.VMEM(relations.shape[::-1], jnp.bfloat16),
            pltpu.VMEM((width, LANES), jnp.bfloat16),
            pltpu.VMEM((2, width, slots * rows), jnp.float32),
            pltpu.VMEM((rows, slots * rows), jnp.float32),
            pltpu.VMEM((width, slots * rows), jnp.bfloat16),
            pltpu.VMEM((width, slots * rows), jnp.bfloat16),
            pltpu.VMEM((rounds, width + SUBLANES, rows), jnp.float32),
            pltpu.VMEM((rounds, width + SUBLANES, rows), jnp.float32),
            pltpu.SemaphoreType.DMA((TABLE_PARTS,)),
            pltpu.SemaphoreType.DMA((rounds, 2)),
            pltpu.SemaphoreType.DMA((rounds, 2)),
        ],
        compiler_params=pltpu.CompilerParams(
            collective_id=0, has_side_effects=True, vmem_limit_bytes=VMEM_BYTES
        ),
    )(
        heads.T,
        tails.T,
        head_acc.reshape(1, rows),
        tail_acc.reshape(1, rows),
        counts.T,
        rel_ids,
        head_edges,
        tail_edges,
        relations.T,
    )
    new_heads, new_tails, new_head_acc, new_tail_acc = pl.pallas_call(
        write_out,
        out_shape=(block, block, line, line),
        in_specs=[hbm] * 4,
        out_specs=(hbm,) * 4,
        scratch_shapes=[
            pltpu.VMEM((width, rows), jnp.float32),
            pltpu.VMEM((width, rows), jnp.float32),
            pltpu.VMEM((1, rows), jnp.float32),
            pltpu.VMEM((1, rows), jnp.float32),
            pltpu.SemaphoreType.DMA((4,)),
            pltpu.SemaphoreType.DMA((4,)),
        ],
        compiler_params=pltpu.CompilerParams(vmem_limit_bytes=VMEM_BYTES),
    )(*results)
    return (new_heads.T, new_tails.T, new_head_acc.reshape(rows), new_tail_acc.reshape(rows))


def solution(mesh):
    both = ("blk", "help")
    in_specs = (
        P(both, None),
        P(both, None),
        P(both),
        P(both),
        P(),
        P(None, both),
        P(None, both, None),
        P(None, both, None, None),
        P(None, both, None, None),
    )
    out_specs = (P(both, None), P(both, None), P(both), P(both))
    return jax.shard_map(
        functools.partial(on_device, mesh.shape["blk"]),
        mesh=mesh,
        in_specs=in_specs,
        out_specs=out_specs,
        check_vma=False,
    )
```

```python
import functools

import jax
import jax.numpy as jnp
from jax import lax
from jax.experimental import pallas as pl
from jax.experimental.pallas import tpu as pltpu
from jax.sharding import PartitionSpec as P

NEG_WEIGHT = 0.0625
LEARN_RATE = 0.1
LANES = 128
SUBLANES = 8
FIRST_PART = 256
TABLE_PARTS = 4
VMEM_BYTES = 60 * 1024 * 1024
NT = (((1,), (1,)), ((), ()))
NN = (((1,), (0,)), ((), ()))


def split(value):
    high = value.astype(jnp.bfloat16)
    return high, (value - high.astype(jnp.float32)).astype(jnp.bfloat16)


def dot(left, right, dims=NN):
    return lax.dot_general(left, right, dims, preferred_element_type=jnp.float32)


def task(s, rows):
    return slice(s * rows, (s + 1) * rows)


def one_hot(index, rows):
    row_of = lax.broadcasted_iota(jnp.int32, (rows, index.shape[1]), 0)
    same = row_of.astype(jnp.bfloat16) == index.astype(jnp.bfloat16)
    return jnp.where(same, jnp.bfloat16(1.0), jnp.bfloat16(0.0))


def label_counts(head_index, tail_index, rows):
    return dot(one_hot(head_index, rows), one_hot(tail_index, rows), NT)


def kernel(
    blk_size,
    heads_ref,
    tails_ref,
    head_acc_ref,
    tail_acc_ref,
    counts_ref,
    rel_ids_ref,
    head_edges_ref,
    tail_edges_ref,
    relations_hbm,
    new_heads_ref,
    new_tails_ref,
    new_head_acc_ref,
    new_tail_acc_ref,
    table,
    gathered,
    gathered_turned,
    turned_high,
    turned_low,
    spread_rel,
    shifted_labels,
    scaled_high,
    scaled_low,
    arrived,
    leaving,
    table_sems,
    send_sem,
    recv_sem,
):
    width, rows = heads_ref.shape
    rounds = counts_ref.shape[1]
    slots = rel_ids_ref.shape[2]
    rels = table.shape[1]
    padded = width + SUBLANES
    parts = ((0, FIRST_PART), (FIRST_PART, padded))
    me = lax.axis_index("blk")

    def device(distance):
        return lax.rem(me + distance + blk_size, blk_size)

    step = pl.cdiv(rels, TABLE_PARTS * 2 * LANES) * 2 * LANES
    table_copies = []
    for at, start in enumerate(range(0, rels, step)):
        lanes = pl.ds(start, min(step, rels - start))
        copy = pltpu.make_async_copy(
            relations_hbm.at[:, lanes], table.at[:, lanes], table_sems.at[at]
        )
        copy.start()
        table_copies.append(copy)

    barrier = pltpu.get_barrier_semaphore()
    partners = (1, -1, rounds - 1, 1 - rounds)
    for distance in partners:
        pl.semaphore_signal(
            barrier,
            inc=1,
            device_id={"blk": device(distance)},
            device_id_type=pl.DeviceIdType.MESH,
        )

    def store_labels(k):
        for s in range(slots):
            at = k * slots + s
            counted = label_counts(head_edges_ref[at], tail_edges_ref[at], rows)
            kept = jnp.where(counts_ref[:, k : k + 1] > s, 1.0, 0.0)
            shifted_labels[task(s, rows), :] = kept * (0.5 * NEG_WEIGHT - counted)

    def gather_relations():
        lane = lax.broadcasted_iota(jnp.int32, (1, LANES), 1)
        wanted = jnp.full((1, LANES), -1, jnp.int32)
        for at in range(rounds * slots):
            rel_id = rel_ids_ref[at // slots, :, at % slots : at % slots + 1]
            wanted = jnp.where(lane == at, rel_id, wanted)
        total = jnp.zeros(gathered.shape, jnp.float32)
        for at, start in enumerate(range(0, rels, step)):
            size = min(step, rels - start)
            rel_of = lax.broadcasted_iota(jnp.int32, (size, LANES), 0) + start
            pick = jnp.where(rel_of == wanted, 1.0, 0.0).astype(jnp.bfloat16)
            table_copies[at].wait()
            total = total + dot(table[:, start : start + size], pick)
        gathered[...] = total.astype(jnp.bfloat16)
        gathered_turned[...] = jnp.transpose(total)

    def store_scaled(k, head_block):
        lane_of = lax.broadcasted_iota(jnp.int32, (LANES, slots * rows), 0)
        task_of = lax.broadcasted_iota(jnp.int32, (LANES, slots * rows), 1) // rows
        pick = jnp.where(lane_of == k * slots + task_of, 1.0, 0.0).astype(jnp.bfloat16)
        spread = dot(gathered[...], pick)
        spread_rel[k % 2] = spread
        for s in range(slots):
            high, low = split(head_block * spread[:, task(s, rows)])
            scaled_high[:, task(s, rows)] = high
            scaled_low[:, task(s, rows)] = low
        head_turned = jnp.transpose(head_block)
        for s in range(slots):
            at = k * slots + s
            high, low = split(head_turned * gathered_turned[at : at + 1, :])
            turned_high[task(s, rows), :] = high
            turned_low[task(s, rows), :] = low

    def state_after(state, grad):
        return state + jnp.sum(grad * grad, axis=0, keepdims=True) * (1.0 / width)

    store_labels(0)
    gather_relations()
    store_scaled(0, heads_ref[...])
    head_state = head_acc_ref[...]
    pl.semaphore_wait(barrier, len(partners))

    copies = []
    for k in range(rounds):
        scores = None
        pieces = []
        for at, (start, stop) in enumerate(parts):
            end = min(stop, width)
            if k == 0:
                piece = tails_ref[start:end, :]
            else:
                copies[2 * (k - 1) + at].wait_recv()
                piece = arrived[k - 1, start:end, :]
            high, low = split(piece)
            wide = dot(turned_high[:, start:end], jnp.concatenate([high, low], axis=1))
            partial = wide[:, :rows] + (wide[:, rows:] + dot(turned_low[:, start:end], high))
            scores = partial if scores is None else scores + partial
            pieces.append(piece)
        tail_state = tail_acc_ref[...] if k == 0 else arrived[k - 1, width : width + 1, :]
        task_of = lax.broadcasted_iota(jnp.int32, (slots * rows, 1), 0) // rows
        active = jnp.where(task_of < counts_ref[:, k : k + 1], 1.0, 0.0)
        weight = active * (0.5 * NEG_WEIGHT)
        coefficient = weight * jnp.tanh(0.5 * scores) + shifted_labels[...]
        high, low = split(coefficient)
        both = dot(scaled_high[...], jnp.concatenate([high, low], axis=1))
        tail_grad = both[:, :rows] + (both[:, rows:] + dot(scaled_low[...], high))
        tail_state = state_after(tail_state, tail_grad)
        rate = LEARN_RATE / jnp.sqrt(tail_state)
        for at, (start, stop) in enumerate(parts):
            end = min(stop, width)
            leaving[k, start:end, :] = pieces[at] - tail_grad[start:end] * rate
            if stop > width:
                leaving[k, width:, :] = jnp.broadcast_to(tail_state, (SUBLANES, rows))
            copy = pltpu.make_async_remote_copy(
                src_ref=leaving.at[k, pl.ds(start, stop - start)],
                dst_ref=arrived.at[k, pl.ds(start, stop - start)],
                send_sem=send_sem.at[k, at],
                recv_sem=recv_sem.at[k, at],
                device_id={"blk": device(1 if k < rounds - 1 else 1 - rounds)},
                device_id_type=pl.DeviceIdType.MESH,
            )
            copy.start()
            copies.append(copy)

        tail_high, tail_low = split(jnp.concatenate(pieces, axis=0))
        wide = jnp.concatenate([tail_high, tail_low, tail_high], axis=1)
        mixed = jnp.concatenate([high, high, low], axis=1)
        weighted = dot(wide, mixed, NT) * spread_rel[k % 2]
        head_grad = weighted[:, task(0, rows)]
        for s in range(1, slots):
            head_grad = head_grad + weighted[:, task(s, rows)]
        old_head = heads_ref[...] if k == 0 else new_heads_ref[...]
        head_state = state_after(head_state, head_grad)
        new_head = old_head - head_grad * (LEARN_RATE / jnp.sqrt(head_state))
        new_heads_ref[...] = new_head
        if k < rounds - 1:
            store_scaled(k + 1, new_head)
            store_labels(k + 1)

    new_head_acc_ref[...] = head_state
    for copy in copies[-2:]:
        copy.wait_recv()
    new_tails_ref[...] = arrived[rounds - 1, :width, :]
    new_tail_acc_ref[...] = arrived[rounds - 1, width : width + 1, :]
    for copy in copies:
        copy.wait_send()


def write_out(*refs):
    count = (len(refs) - 2) // 3
    sems_in, sems_out = refs[-2:]
    copies_in = []
    copies_out = []
    for at in range(count):
        near = refs[2 * count + at]
        copies_in.append(pltpu.make_async_copy(refs[at], near, sems_in.at[at]))
        copies_out.append(pltpu.make_async_copy(near, refs[count + at], sems_out.at[at]))
        copies_in[at].start()
    for at in range(count):
        copies_in[at].wait()
        copies_out[at].start()
    for copy in copies_out:
        copy.wait()


def on_device(
    blk_size, heads, tails, head_acc, tail_acc, relations, counts, rel_ids, head_edges, tail_edges
):
    rows, width = heads.shape
    rounds, _, slots, edges = head_edges.shape
    vmem = pl.BlockSpec(memory_space=pltpu.VMEM)
    hbm = pl.BlockSpec(memory_space=pltpu.HBM)
    block = jax.ShapeDtypeStruct((width, rows), jnp.float32)
    line = jax.ShapeDtypeStruct((1, rows), jnp.float32)
    head_edges = head_edges.reshape(rounds * slots, 1, edges)
    tail_edges = tail_edges.reshape(rounds * slots, 1, edges)
    results = pl.pallas_call(
        functools.partial(kernel, blk_size),
        out_shape=(block, block, line, line),
        in_specs=[vmem] * 8 + [hbm],
        out_specs=(vmem,) * 4,
        scratch_shapes=[
            pltpu.VMEM(relations.shape[::-1], jnp.bfloat16),
            pltpu.VMEM((width, LANES), jnp.bfloat16),
            pltpu.VMEM((LANES, width), jnp.float32),
            pltpu.VMEM((slots * rows, width), jnp.bfloat16),
            pltpu.VMEM((slots * rows, width), jnp.bfloat16),
            pltpu.VMEM((2, width, slots * rows), jnp.float32),
            pltpu.VMEM((slots * rows, rows), jnp.float32),
            pltpu.VMEM((width, slots * rows), jnp.bfloat16),
            pltpu.VMEM((width, slots * rows), jnp.bfloat16),
            pltpu.VMEM((rounds, width + SUBLANES, rows), jnp.float32),
            pltpu.VMEM((rounds, width + SUBLANES, rows), jnp.float32),
            pltpu.SemaphoreType.DMA((TABLE_PARTS,)),
            pltpu.SemaphoreType.DMA((rounds, 2)),
            pltpu.SemaphoreType.DMA((rounds, 2)),
        ],
        compiler_params=pltpu.CompilerParams(
            collective_id=0, has_side_effects=True, vmem_limit_bytes=VMEM_BYTES
        ),
    )(
        heads.T,
        tails.T,
        head_acc.reshape(1, rows),
        tail_acc.reshape(1, rows),
        counts.T,
        rel_ids,
        head_edges,
        tail_edges,
        relations.T,
    )
    new_heads, new_tails, new_head_acc, new_tail_acc = pl.pallas_call(
        write_out,
        out_shape=(block, block, line, line),
        in_specs=[hbm] * 4,
        out_specs=(hbm,) * 4,
        scratch_shapes=[
            pltpu.VMEM((width, rows), jnp.float32),
            pltpu.VMEM((width, rows), jnp.float32),
            pltpu.VMEM((1, rows), jnp.float32),
            pltpu.VMEM((1, rows), jnp.float32),
            pltpu.SemaphoreType.DMA((4,)),
            pltpu.SemaphoreType.DMA((4,)),
        ],
        compiler_params=pltpu.CompilerParams(vmem_limit_bytes=VMEM_BYTES),
    )(*results)
    return (new_heads.T, new_tails.T, new_head_acc.reshape(rows), new_tail_acc.reshape(rows))


def solution(mesh):
    both = ("blk", "help")
    in_specs = (
        P(both, None),
        P(both, None),
        P(both),
        P(both),
        P(),
        P(None, both),
        P(None, both, None),
        P(None, both, None, None),
        P(None, both, None, None),
    )
    out_specs = (P(both, None), P(both, None), P(both), P(both))
    return jax.shard_map(
        functools.partial(on_device, mesh.shape["blk"]),
        mesh=mesh,
        in_specs=in_specs,
        out_specs=out_specs,
        check_vma=False,
    )
```

```python
import functools

import jax
import jax.numpy as jnp
from jax import lax
from jax.experimental import pallas as pl
from jax.experimental.pallas import tpu as pltpu
from jax.sharding import PartitionSpec as P

NEG_WEIGHT = 0.0625
LEARN_RATE = 0.1
LANES = 128
SUBLANES = 8
FIRST_PART = 256
TABLE_PARTS = 4
VMEM_BYTES = 60 * 1024 * 1024
NT = (((1,), (1,)), ((), ()))
NN = (((1,), (0,)), ((), ()))


def split(value):
    high = value.astype(jnp.bfloat16)
    return high, (value - high.astype(jnp.float32)).astype(jnp.bfloat16)


def dot(left, right, dims=NN):
    return lax.dot_general(left, right, dims, preferred_element_type=jnp.float32)


def task(s, rows):
    return slice(s * rows, (s + 1) * rows)


def one_hot(index, rows):
    row_of = lax.broadcasted_iota(jnp.int32, (rows, index.shape[1]), 0)
    same = row_of.astype(jnp.bfloat16) == index.astype(jnp.bfloat16)
    return jnp.where(same, jnp.bfloat16(1.0), jnp.bfloat16(0.0))


def label_counts(head_index, tail_index, rows):
    return dot(one_hot(head_index, rows), one_hot(tail_index, rows), NT)


def kernel(
    blk_size,
    heads_hbm,
    tails_hbm,
    head_acc_hbm,
    tail_acc_hbm,
    counts_hbm,
    rel_ids_hbm,
    head_edges_hbm,
    tail_edges_hbm,
    relations_hbm,
    new_heads_hbm,
    new_tails_hbm,
    new_head_acc_hbm,
    new_tail_acc_hbm,
    heads_ref,
    tails_ref,
    head_acc_ref,
    tail_acc_ref,
    counts_ref,
    rel_ids_ref,
    head_edges_ref,
    tail_edges_ref,
    new_heads_ref,
    new_head_acc_ref,
    new_tail_acc_ref,
    table,
    gathered,
    gathered_turned,
    turned_high,
    turned_low,
    spread_rel,
    shifted_labels,
    scaled_high,
    scaled_low,
    arrived,
    leaving,
    input_sems,
    output_sems,
    table_sems,
    send_sem,
    recv_sem,
):
    width, rows = heads_ref.shape
    rounds = counts_ref.shape[1]
    slots = rel_ids_ref.shape[2]
    rels = table.shape[1]
    padded = width + SUBLANES
    parts = ((0, FIRST_PART), (FIRST_PART, padded))
    me = lax.axis_index("blk")

    def device(distance):
        return lax.rem(me + distance + blk_size, blk_size)

    inputs = (
        (rel_ids_hbm, rel_ids_ref),
        (counts_hbm, counts_ref),
        (head_edges_hbm, head_edges_ref),
        (tail_edges_hbm, tail_edges_ref),
        (heads_hbm, heads_ref),
        (tails_hbm, tails_ref),
        (head_acc_hbm, head_acc_ref),
        (tail_acc_hbm, tail_acc_ref),
    )
    input_copies = []
    for at, (source, target) in enumerate(inputs):
        copy = pltpu.make_async_copy(source, target, input_sems.at[at])
        copy.start()
        input_copies.append(copy)

    step = pl.cdiv(rels, TABLE_PARTS * 2 * LANES) * 2 * LANES
    table_copies = []
    for at, start in enumerate(range(0, rels, step)):
        lanes = pl.ds(start, min(step, rels - start))
        copy = pltpu.make_async_copy(
            relations_hbm.at[:, lanes], table.at[:, lanes], table_sems.at[at]
        )
        copy.start()
        table_copies.append(copy)

    barrier = pltpu.get_barrier_semaphore()
    partners = (1, -1, rounds - 1, 1 - rounds)
    for distance in partners:
        pl.semaphore_signal(
            barrier,
            inc=1,
            device_id={"blk": device(distance)},
            device_id_type=pl.DeviceIdType.MESH,
        )

    def store_labels(k):
        for s in range(slots):
            at = k * slots + s
            counted = label_counts(head_edges_ref[at], tail_edges_ref[at], rows)
            kept = jnp.where(counts_ref[:, k : k + 1] > s, 1.0, 0.0)
            shifted_labels[task(s, rows), :] = kept * (0.5 * NEG_WEIGHT - counted)

    def gather_relations():
        lane = lax.broadcasted_iota(jnp.int32, (1, LANES), 1)
        wanted = jnp.full((1, LANES), -1, jnp.int32)
        for at in range(rounds * slots):
            rel_id = rel_ids_ref[at // slots, :, at % slots : at % slots + 1]
            wanted = jnp.where(lane == at, rel_id, wanted)
        total = jnp.zeros(gathered.shape, jnp.float32)
        for at, start in enumerate(range(0, rels, step)):
            size = min(step, rels - start)
            rel_of = lax.broadcasted_iota(jnp.int32, (size, LANES), 0) + start
            pick = jnp.where(rel_of == wanted, 1.0, 0.0).astype(jnp.bfloat16)
            table_copies[at].wait()
            total = total + dot(table[:, start : start + size], pick)
        gathered[...] = total.astype(jnp.bfloat16)
        gathered_turned[...] = jnp.transpose(total)

    def store_scaled(k, head_block):
        lane_of = lax.broadcasted_iota(jnp.int32, (LANES, slots * rows), 0)
        task_of = lax.broadcasted_iota(jnp.int32, (LANES, slots * rows), 1) // rows
        pick = jnp.where(lane_of == k * slots + task_of, 1.0, 0.0).astype(jnp.bfloat16)
        spread = dot(gathered[...], pick)
        spread_rel[k % 2] = spread
        for s in range(slots):
            high, low = split(head_block * spread[:, task(s, rows)])
            scaled_high[:, task(s, rows)] = high
            scaled_low[:, task(s, rows)] = low
        head_turned = jnp.transpose(head_block)
        for s in range(slots):
            at = k * slots + s
            high, low = split(head_turned * gathered_turned[at : at + 1, :])
            turned_high[task(s, rows), :] = high
            turned_low[task(s, rows), :] = low

    def state_after(state, grad):
        return state + jnp.sum(grad * grad, axis=0, keepdims=True) * (1.0 / width)

    for copy in input_copies[:4]:
        copy.wait()
    store_labels(0)
    gather_relations()
    for copy in input_copies[4:]:
        copy.wait()
    store_scaled(0, heads_ref[...])
    head_state = head_acc_ref[...]
    pl.semaphore_wait(barrier, len(partners))

    copies = []
    for k in range(rounds):
        scores = None
        pieces = []
        for at, (start, stop) in enumerate(parts):
            end = min(stop, width)
            if k == 0:
                piece = tails_ref[start:end, :]
            else:
                copies[2 * (k - 1) + at].wait_recv()
                piece = arrived[k - 1, start:end, :]
            high, low = split(piece)
            wide = dot(turned_high[:, start:end], jnp.concatenate([high, low], axis=1))
            partial = wide[:, :rows] + (wide[:, rows:] + dot(turned_low[:, start:end], high))
            scores = partial if scores is None else scores + partial
            pieces.append(piece)
        tail_state = tail_acc_ref[...] if k == 0 else arrived[k - 1, width : width + 1, :]
        task_of = lax.broadcasted_iota(jnp.int32, (slots * rows, 1), 0) // rows
        active = jnp.where(task_of < counts_ref[:, k : k + 1], 1.0, 0.0)
        weight = active * (0.5 * NEG_WEIGHT)
        coefficient = weight * jnp.tanh(0.5 * scores) + shifted_labels[...]
        high, low = split(coefficient)
        both = dot(scaled_high[...], jnp.concatenate([high, low], axis=1))
        tail_grad = both[:, :rows] + (both[:, rows:] + dot(scaled_low[...], high))
        tail_state = state_after(tail_state, tail_grad)
        rate = LEARN_RATE / jnp.sqrt(tail_state)
        for at, (start, stop) in enumerate(parts):
            end = min(stop, width)
            leaving[k, start:end, :] = pieces[at] - tail_grad[start:end] * rate
            if stop > width:
                leaving[k, width:, :] = jnp.broadcast_to(tail_state, (SUBLANES, rows))
            copy = pltpu.make_async_remote_copy(
                src_ref=leaving.at[k, pl.ds(start, stop - start)],
                dst_ref=arrived.at[k, pl.ds(start, stop - start)],
                send_sem=send_sem.at[k, at],
                recv_sem=recv_sem.at[k, at],
                device_id={"blk": device(1 if k < rounds - 1 else 1 - rounds)},
                device_id_type=pl.DeviceIdType.MESH,
            )
            copy.start()
            copies.append(copy)

        tail_high, tail_low = split(jnp.concatenate(pieces, axis=0))
        wide = jnp.concatenate([tail_high, tail_low, tail_high], axis=1)
        mixed = jnp.concatenate([high, high, low], axis=1)
        weighted = dot(wide, mixed, NT) * spread_rel[k % 2]
        head_grad = weighted[:, task(0, rows)]
        for s in range(1, slots):
            head_grad = head_grad + weighted[:, task(s, rows)]
        old_head = heads_ref[...] if k == 0 else new_heads_ref[...]
        head_state = state_after(head_state, head_grad)
        new_head = old_head - head_grad * (LEARN_RATE / jnp.sqrt(head_state))
        new_heads_ref[...] = new_head
        if k < rounds - 1:
            store_scaled(k + 1, new_head)
            store_labels(k + 1)

    new_head_acc_ref[...] = head_state
    outputs = [(new_heads_ref, new_heads_hbm), (new_head_acc_ref, new_head_acc_hbm)]
    for start, stop in parts:
        span = pl.ds(start, min(stop, width) - start)
        outputs.append((arrived.at[rounds - 1, span], new_tails_hbm.at[span]))
    outputs.append((new_tail_acc_ref, new_tail_acc_hbm))
    output_copies = [
        pltpu.make_async_copy(source, target, output_sems.at[at])
        for at, (source, target) in enumerate(outputs)
    ]
    output_copies[0].start()
    output_copies[1].start()
    copies[-2].wait_recv()
    output_copies[2].start()
    copies[-1].wait_recv()
    output_copies[3].start()
    new_tail_acc_ref[...] = arrived[rounds - 1, width : width + 1, :]
    output_copies[4].start()
    for copy in output_copies:
        copy.wait()
    for copy in copies:
        copy.wait_send()


def write_out(*refs):
    count = (len(refs) - 2) // 3
    sems_in, sems_out = refs[-2:]
    copies_in = []
    copies_out = []
    for at in range(count):
        near = refs[2 * count + at]
        copies_in.append(pltpu.make_async_copy(refs[at], near, sems_in.at[at]))
        copies_out.append(pltpu.make_async_copy(near, refs[count + at], sems_out.at[at]))
        copies_in[at].start()
    for at in range(count):
        copies_in[at].wait()
        copies_out[at].start()
    for copy in copies_out:
        copy.wait()


def on_device(
    blk_size, heads, tails, head_acc, tail_acc, relations, counts, rel_ids, head_edges, tail_edges
):
    rows, width = heads.shape
    rounds, _, slots, edges = head_edges.shape
    hbm = pl.BlockSpec(memory_space=pltpu.HBM)
    block = jax.ShapeDtypeStruct((width, rows), jnp.float32)
    line = jax.ShapeDtypeStruct((1, rows), jnp.float32)
    head_edges = head_edges.reshape(rounds * slots, 1, edges)
    tail_edges = tail_edges.reshape(rounds * slots, 1, edges)
    results = pl.pallas_call(
        functools.partial(kernel, blk_size),
        out_shape=(block, block, line, line),
        in_specs=[hbm] * 9,
        out_specs=(hbm,) * 4,
        scratch_shapes=[
            pltpu.VMEM((width, rows), jnp.float32),
            pltpu.VMEM((width, rows), jnp.float32),
            pltpu.VMEM((1, rows), jnp.float32),
            pltpu.VMEM((1, rows), jnp.float32),
            pltpu.VMEM((1, rounds), jnp.int32),
            pltpu.VMEM(rel_ids.shape, jnp.int32),
            pltpu.VMEM(head_edges.shape, jnp.int32),
            pltpu.VMEM(tail_edges.shape, jnp.int32),
            pltpu.VMEM((width, rows), jnp.float32),
            pltpu.VMEM((1, rows), jnp.float32),
            pltpu.VMEM((1, rows), jnp.float32),
            pltpu.VMEM(relations.shape[::-1], jnp.bfloat16),
            pltpu.VMEM((width, LANES), jnp.bfloat16),
            pltpu.VMEM((LANES, width), jnp.float32),
            pltpu.VMEM((slots * rows, width), jnp.bfloat16),
            pltpu.VMEM((slots * rows, width), jnp.bfloat16),
            pltpu.VMEM((2, width, slots * rows), jnp.float32),
            pltpu.VMEM((slots * rows, rows), jnp.float32),
            pltpu.VMEM((width, slots * rows), jnp.bfloat16),
            pltpu.VMEM((width, slots * rows), jnp.bfloat16),
            pltpu.VMEM((rounds, width + SUBLANES, rows), jnp.float32),
            pltpu.VMEM((rounds, width + SUBLANES, rows), jnp.float32),
            pltpu.SemaphoreType.DMA((8,)),
            pltpu.SemaphoreType.DMA((5,)),
            pltpu.SemaphoreType.DMA((TABLE_PARTS,)),
            pltpu.SemaphoreType.DMA((rounds, 2)),
            pltpu.SemaphoreType.DMA((rounds, 2)),
        ],
        compiler_params=pltpu.CompilerParams(
            collective_id=0, has_side_effects=True, vmem_limit_bytes=VMEM_BYTES
        ),
    )(
        heads.T,
        tails.T,
        head_acc.reshape(1, rows),
        tail_acc.reshape(1, rows),
        counts.T,
        rel_ids,
        head_edges,
        tail_edges,
        relations.T,
    )
    new_heads, new_tails, new_head_acc, new_tail_acc = pl.pallas_call(
        write_out,
        out_shape=(block, block, line, line),
        in_specs=[hbm] * 4,
        out_specs=(hbm,) * 4,
        scratch_shapes=[
            pltpu.VMEM((width, rows), jnp.float32),
            pltpu.VMEM((width, rows), jnp.float32),
            pltpu.VMEM((1, rows), jnp.float32),
            pltpu.VMEM((1, rows), jnp.float32),
            pltpu.SemaphoreType.DMA((4,)),
            pltpu.SemaphoreType.DMA((4,)),
        ],
        compiler_params=pltpu.CompilerParams(vmem_limit_bytes=VMEM_BYTES),
    )(*results)
    return (new_heads.T, new_tails.T, new_head_acc.reshape(rows), new_tail_acc.reshape(rows))


def solution(mesh):
    both = ("blk", "help")
    in_specs = (
        P(both, None),
        P(both, None),
        P(both),
        P(both),
        P(),
        P(None, both),
        P(None, both, None),
        P(None, both, None, None),
        P(None, both, None, None),
    )
    out_specs = (P(both, None), P(both, None), P(both), P(both))
    return jax.shard_map(
        functools.partial(on_device, mesh.shape["blk"]),
        mesh=mesh,
        in_specs=in_specs,
        out_specs=out_specs,
        check_vma=False,
    )
```

```python
import functools

import jax
import jax.numpy as jnp
from jax import lax
from jax.experimental import pallas as pl
from jax.experimental.pallas import tpu as pltpu
from jax.sharding import PartitionSpec as P

NEG_WEIGHT = 0.0625
LEARN_RATE = 0.1
LANES = 128
SUBLANES = 8
FIRST_PART = 256
TABLE_PARTS = 8
VMEM_BYTES = 60 * 1024 * 1024
NT = (((1,), (1,)), ((), ()))
NN = (((1,), (0,)), ((), ()))


def split(value):
    high = value.astype(jnp.bfloat16)
    return high, (value - high.astype(jnp.float32)).astype(jnp.bfloat16)


def dot(left, right, dims=NN):
    return lax.dot_general(left, right, dims, preferred_element_type=jnp.float32)


def task(s, rows):
    return slice(s * rows, (s + 1) * rows)


def one_hot(index, rows):
    row_of = lax.broadcasted_iota(jnp.int32, (rows, index.shape[1]), 0)
    same = row_of.astype(jnp.bfloat16) == index.astype(jnp.bfloat16)
    return jnp.where(same, jnp.bfloat16(1.0), jnp.bfloat16(0.0))


def label_counts(head_index, tail_index, rows):
    return dot(one_hot(head_index, rows), one_hot(tail_index, rows), NT)


def kernel(
    blk_size,
    heads_hbm,
    tails_hbm,
    head_acc_hbm,
    tail_acc_hbm,
    counts_hbm,
    rel_ids_hbm,
    head_edges_hbm,
    tail_edges_hbm,
    relations_hbm,
    new_heads_hbm,
    new_tails_hbm,
    new_head_acc_hbm,
    new_tail_acc_hbm,
    heads_ref,
    tails_ref,
    head_acc_ref,
    tail_acc_ref,
    counts_ref,
    rel_ids_ref,
    head_edges_ref,
    tail_edges_ref,
    new_heads_ref,
    new_head_acc_ref,
    new_tail_acc_ref,
    table,
    gathered,
    gathered_turned,
    turned_high,
    turned_low,
    spread_rel,
    shifted_labels,
    scaled_high,
    scaled_low,
    arrived,
    leaving,
    input_sems,
    output_sems,
    table_sems,
    send_sem,
    recv_sem,
):
    width, rows = heads_ref.shape
    rounds = counts_ref.shape[1]
    slots = rel_ids_ref.shape[2]
    rels = table.shape[1]
    padded = width + SUBLANES
    parts = ((0, FIRST_PART), (FIRST_PART, padded))
    me = lax.axis_index("blk")

    def device(distance):
        return lax.rem(me + distance + blk_size, blk_size)

    inputs = (
        (rel_ids_hbm, rel_ids_ref),
        (counts_hbm, counts_ref),
        (head_edges_hbm, head_edges_ref),
        (tail_edges_hbm, tail_edges_ref),
        (heads_hbm, heads_ref),
        (tails_hbm, tails_ref),
        (head_acc_hbm, head_acc_ref),
        (tail_acc_hbm, tail_acc_ref),
    )
    input_copies = []
    for at, (source, target) in enumerate(inputs):
        copy = pltpu.make_async_copy(source, target, input_sems.at[at])
        copy.start()
        input_copies.append(copy)

    step = pl.cdiv(rels, TABLE_PARTS * 2 * LANES) * 2 * LANES
    table_copies = []
    for at, start in enumerate(range(0, rels, step)):
        lanes = pl.ds(start, min(step, rels - start))
        copy = pltpu.make_async_copy(
            relations_hbm.at[:, lanes], table.at[:, lanes], table_sems.at[at]
        )
        copy.start()
        table_copies.append(copy)

    barrier = pltpu.get_barrier_semaphore()
    partners = (1, -1, rounds - 1, 1 - rounds)
    for distance in partners:
        pl.semaphore_signal(
            barrier,
            inc=1,
            device_id={"blk": device(distance)},
            device_id_type=pl.DeviceIdType.MESH,
        )

    def store_labels(k):
        for s in range(slots):
            at = k * slots + s
            counted = label_counts(head_edges_ref[at], tail_edges_ref[at], rows)
            kept = jnp.where(counts_ref[:, k : k + 1] > s, 1.0, 0.0)
            shifted_labels[task(s, rows), :] = kept * (0.5 * NEG_WEIGHT - counted)

    def gather_relations():
        lane = lax.broadcasted_iota(jnp.int32, (1, LANES), 1)
        wanted = jnp.full((1, LANES), -1, jnp.int32)
        for at in range(rounds * slots):
            rel_id = rel_ids_ref[at // slots, :, at % slots : at % slots + 1]
            wanted = jnp.where(lane == at, rel_id, wanted)
        total = jnp.zeros(gathered.shape, jnp.float32)
        for at, start in enumerate(range(0, rels, step)):
            size = min(step, rels - start)
            rel_of = lax.broadcasted_iota(jnp.int32, (size, LANES), 0) + start
            pick = jnp.where(rel_of == wanted, 1.0, 0.0).astype(jnp.bfloat16)
            table_copies[at].wait()
            total = total + dot(table[:, start : start + size], pick)
        gathered[...] = total.astype(jnp.bfloat16)
        gathered_turned[...] = jnp.transpose(total)

    def store_scaled(k, head_block):
        lane_of = lax.broadcasted_iota(jnp.int32, (LANES, slots * rows), 0)
        task_of = lax.broadcasted_iota(jnp.int32, (LANES, slots * rows), 1) // rows
        pick = jnp.where(lane_of == k * slots + task_of, 1.0, 0.0).astype(jnp.bfloat16)
        spread = dot(gathered[...], pick)
        spread_rel[k % 2] = spread
        for s in range(slots):
            high, low = split(head_block * spread[:, task(s, rows)])
            scaled_high[:, task(s, rows)] = high
            scaled_low[:, task(s, rows)] = low
        head_turned = jnp.transpose(head_block)
        for s in range(slots):
            at = k * slots + s
            high, low = split(head_turned * gathered_turned[at : at + 1, :])
            turned_high[task(s, rows), :] = high
            turned_low[task(s, rows), :] = low

    def state_after(state, grad):
        return state + jnp.sum(grad * grad, axis=0, keepdims=True) * (1.0 / width)

    for copy in input_copies[:4]:
        copy.wait()
    store_labels(0)
    gather_relations()
    for copy in input_copies[4:]:
        copy.wait()
    store_scaled(0, heads_ref[...])
    head_state = head_acc_ref[...]
    pl.semaphore_wait(barrier, len(partners))

    copies = []
    for k in range(rounds):
        scores = None
        pieces = []
        for at, (start, stop) in enumerate(parts):
            end = min(stop, width)
            if k == 0:
                piece = tails_ref[start:end, :]
            else:
                copies[2 * (k - 1) + at].wait_recv()
                piece = arrived[k - 1, start:end, :]
            high, low = split(piece)
            wide = dot(turned_high[:, start:end], jnp.concatenate([high, low], axis=1))
            partial = wide[:, :rows] + (wide[:, rows:] + dot(turned_low[:, start:end], high))
            scores = partial if scores is None else scores + partial
            pieces.append(piece)
        tail_state = tail_acc_ref[...] if k == 0 else arrived[k - 1, width : width + 1, :]
        task_of = lax.broadcasted_iota(jnp.int32, (slots * rows, 1), 0) // rows
        active = jnp.where(task_of < counts_ref[:, k : k + 1], 1.0, 0.0)
        weight = active * (0.5 * NEG_WEIGHT)
        coefficient = weight * jnp.tanh(0.5 * scores) + shifted_labels[...]
        high, low = split(coefficient)
        both = dot(scaled_high[...], jnp.concatenate([high, low], axis=1))
        tail_grad = both[:, :rows] + (both[:, rows:] + dot(scaled_low[...], high))
        tail_state = state_after(tail_state, tail_grad)
        rate = LEARN_RATE / jnp.sqrt(tail_state)
        for at, (start, stop) in enumerate(parts):
            end = min(stop, width)
            leaving[k, start:end, :] = pieces[at] - tail_grad[start:end] * rate
            if stop > width:
                leaving[k, width:, :] = jnp.broadcast_to(tail_state, (SUBLANES, rows))
            copy = pltpu.make_async_remote_copy(
                src_ref=leaving.at[k, pl.ds(start, stop - start)],
                dst_ref=arrived.at[k, pl.ds(start, stop - start)],
                send_sem=send_sem.at[k, at],
                recv_sem=recv_sem.at[k, at],
                device_id={"blk": device(1 if k < rounds - 1 else 1 - rounds)},
                device_id_type=pl.DeviceIdType.MESH,
            )
            copy.start()
            copies.append(copy)

        tail_high, tail_low = split(jnp.concatenate(pieces, axis=0))
        wide = jnp.concatenate([tail_high, tail_low, tail_high], axis=1)
        mixed = jnp.concatenate([high, high, low], axis=1)
        weighted = dot(wide, mixed, NT) * spread_rel[k % 2]
        head_grad = weighted[:, task(0, rows)]
        for s in range(1, slots):
            head_grad = head_grad + weighted[:, task(s, rows)]
        old_head = heads_ref[...] if k == 0 else new_heads_ref[...]
        head_state = state_after(head_state, head_grad)
        new_head = old_head - head_grad * (LEARN_RATE / jnp.sqrt(head_state))
        new_heads_ref[...] = new_head
        if k < rounds - 1:
            store_scaled(k + 1, new_head)
            store_labels(k + 1)

    new_head_acc_ref[...] = head_state
    outputs = [(new_heads_ref, new_heads_hbm), (new_head_acc_ref, new_head_acc_hbm)]
    for start, stop in parts:
        span = pl.ds(start, min(stop, width) - start)
        outputs.append((arrived.at[rounds - 1, span], new_tails_hbm.at[span]))
    outputs.append((new_tail_acc_ref, new_tail_acc_hbm))
    output_copies = [
        pltpu.make_async_copy(source, target, output_sems.at[at])
        for at, (source, target) in enumerate(outputs)
    ]
    output_copies[0].start()
    output_copies[1].start()
    copies[-2].wait_recv()
    output_copies[2].start()
    copies[-1].wait_recv()
    output_copies[3].start()
    new_tail_acc_ref[...] = arrived[rounds - 1, width : width + 1, :]
    output_copies[4].start()
    for copy in output_copies:
        copy.wait()
    for copy in copies:
        copy.wait_send()


def write_out(*refs):
    count = (len(refs) - 2) // 3
    sems_in, sems_out = refs[-2:]
    copies_in = []
    copies_out = []
    for at in range(count):
        near = refs[2 * count + at]
        copies_in.append(pltpu.make_async_copy(refs[at], near, sems_in.at[at]))
        copies_out.append(pltpu.make_async_copy(near, refs[count + at], sems_out.at[at]))
        copies_in[at].start()
    for at in range(count):
        copies_in[at].wait()
        copies_out[at].start()
    for copy in copies_out:
        copy.wait()


def on_device(
    blk_size, heads, tails, head_acc, tail_acc, relations, counts, rel_ids, head_edges, tail_edges
):
    rows, width = heads.shape
    rounds, _, slots, edges = head_edges.shape
    hbm = pl.BlockSpec(memory_space=pltpu.HBM)
    block = jax.ShapeDtypeStruct((width, rows), jnp.float32)
    line = jax.ShapeDtypeStruct((1, rows), jnp.float32)
    head_edges = head_edges.reshape(rounds * slots, 1, edges)
    tail_edges = tail_edges.reshape(rounds * slots, 1, edges)
    results = pl.pallas_call(
        functools.partial(kernel, blk_size),
        out_shape=(block, block, line, line),
        in_specs=[hbm] * 9,
        out_specs=(hbm,) * 4,
        scratch_shapes=[
            pltpu.VMEM((width, rows), jnp.float32),
            pltpu.VMEM((width, rows), jnp.float32),
            pltpu.VMEM((1, rows), jnp.float32),
            pltpu.VMEM((1, rows), jnp.float32),
            pltpu.VMEM((1, rounds), jnp.int32),
            pltpu.VMEM(rel_ids.shape, jnp.int32),
            pltpu.VMEM(head_edges.shape, jnp.int32),
            pltpu.VMEM(tail_edges.shape, jnp.int32),
            pltpu.VMEM((width, rows), jnp.float32),
            pltpu.VMEM((1, rows), jnp.float32),
            pltpu.VMEM((1, rows), jnp.float32),
            pltpu.VMEM(relations.shape[::-1], jnp.bfloat16),
            pltpu.VMEM((width, LANES), jnp.bfloat16),
            pltpu.VMEM((LANES, width), jnp.float32),
            pltpu.VMEM((slots * rows, width), jnp.bfloat16),
            pltpu.VMEM((slots * rows, width), jnp.bfloat16),
            pltpu.VMEM((2, width, slots * rows), jnp.float32),
            pltpu.VMEM((slots * rows, rows), jnp.float32),
            pltpu.VMEM((width, slots * rows), jnp.bfloat16),
            pltpu.VMEM((width, slots * rows), jnp.bfloat16),
            pltpu.VMEM((rounds, width + SUBLANES, rows), jnp.float32),
            pltpu.VMEM((rounds, width + SUBLANES, rows), jnp.float32),
            pltpu.SemaphoreType.DMA((8,)),
            pltpu.SemaphoreType.DMA((5,)),
            pltpu.SemaphoreType.DMA((TABLE_PARTS,)),
            pltpu.SemaphoreType.DMA((rounds, 2)),
            pltpu.SemaphoreType.DMA((rounds, 2)),
        ],
        compiler_params=pltpu.CompilerParams(
            collective_id=0, has_side_effects=True, vmem_limit_bytes=VMEM_BYTES
        ),
    )(
        heads.T,
        tails.T,
        head_acc.reshape(1, rows),
        tail_acc.reshape(1, rows),
        counts.T,
        rel_ids,
        head_edges,
        tail_edges,
        relations.T,
    )
    new_heads, new_tails, new_head_acc, new_tail_acc = pl.pallas_call(
        write_out,
        out_shape=(block, block, line, line),
        in_specs=[hbm] * 4,
        out_specs=(hbm,) * 4,
        scratch_shapes=[
            pltpu.VMEM((width, rows), jnp.float32),
            pltpu.VMEM((width, rows), jnp.float32),
            pltpu.VMEM((1, rows), jnp.float32),
            pltpu.VMEM((1, rows), jnp.float32),
            pltpu.SemaphoreType.DMA((4,)),
            pltpu.SemaphoreType.DMA((4,)),
        ],
        compiler_params=pltpu.CompilerParams(vmem_limit_bytes=VMEM_BYTES),
    )(*results)
    return (new_heads.T, new_tails.T, new_head_acc.reshape(rows), new_tail_acc.reshape(rows))


def solution(mesh):
    both = ("blk", "help")
    in_specs = (
        P(both, None),
        P(both, None),
        P(both),
        P(both),
        P(),
        P(None, both),
        P(None, both, None),
        P(None, both, None, None),
        P(None, both, None, None),
    )
    out_specs = (P(both, None), P(both, None), P(both), P(both))
    return jax.shard_map(
        functools.partial(on_device, mesh.shape["blk"]),
        mesh=mesh,
        in_specs=in_specs,
        out_specs=out_specs,
        check_vma=False,
    )
```
